32 devices in a mesh: groups: 2 (over x), seq: 8 (over z, y), mp: 2 (over core).
Axes of the slice: x: 2, y: 2, z: 4, core: 2. Of those that a mesh axis runs over, the one named last changes fastest.
Arguments:
- queries: bfloat16 [8192, 4096], P(('groups', 'seq'), 'mp'), parts along dimension 0, may hold values from -6 to 6
- keys: bfloat16 [8192, 512], P(('groups', 'seq'), 'mp'), parts along dimension 0, may hold values from -6 to 6
- values: bfloat16 [8192, 512], P(('groups', 'seq'), 'mp'), parts along dimension 0, may hold values from -6 to 6
- feat_weight: bfloat16 [32, 128, 128], P('mp'), may hold values from -0.5 to 0.5
- head_gain: float32 [4096], P('mp'), may hold values from 0.1 to 1.9
- out_weight: bfloat16 [4096, 4096], P('mp'), may hold values from -0.09375 to 0.09375
Outputs:
- mixed: bfloat16 [8192, 4096], P(('groups', 'seq', 'mp')), parts along dimension 0
The draws below stay inside these ranges and needn't reach their ends.
There are 2 independent parts, one for each index of `groups`. The reference program is written for one: setup_inputs(seed, part) draws one part's arguments, and reference() takes and returns one part's arrays. A program takes and returns all parts, laid end to end along the dimension named above; an argument that names none is the same for every part. Nothing has to cross between parts.
All inputs are finite; a program needn't handle non-finite values.
Results may differ from the reference program's by a relative error of at most 0.0083.
Values sent between devices are 32-bit elements; how exact they have to be, the bound alone decides.
A program may use at most 128 MiB of HBM per device.

```python
import jax
import jax.numpy as jnp
from jax import lax

HD = 128
HEADS = 32
KVH = 4
DOUT = 4096
TOK_DEV = 512
TOKENS = 4096
N_SEQ = 8


def draw_values(key, part):
    width = KVH * HD
    half_rows = TOKENS // 2
    first_key, second_key = jax.random.split(key, 2)
    base = jax.random.truncated_normal(first_key, -5.0, 5.0, (half_rows, width), jnp.float32)
    jitter = jax.random.truncated_normal(second_key, -4.0, 4.0, (half_rows, width), jnp.float32)
    even_rows = base
    odd_rows = 0.25 * jitter - base
    paired = jnp.stack([even_rows, odd_rows], axis=1)
    return paired.reshape(TOKENS, width).astype(jnp.bfloat16)


def block_scale(stream_key, dims, shards, low, top_value):
    def one(axis_at, parts):
        heights = jax.random.uniform(jax.random.fold_in(jax.random.fold_in(stream_key, 6), axis_at), (parts,), jnp.float32, low / len(shards), top_value / len(shards))
        return jnp.repeat(jnp.exp(heights), dims[axis_at] // parts).reshape((-1,) + (1,) * (len(dims) - axis_at - 1))

    loudness = one(*shards[0])
    for cut in shards[1:]:
        loudness = loudness * one(*cut)
    return loudness


def scatter_about(own_key, shape, deviation, limit, cuts=(), held_as=jnp.bfloat16):
    array = jax.random.normal(own_key, shape, jnp.float32) * deviation
    if len(cuts) > 0:
        array = block_scale(own_key, shape, cuts, -0.22, 0.18) * array
    return jnp.clip(array, min=-limit, max=limit).astype(held_as)


def setup_inputs(seed: int = 0, part: int = 0) -> dict:
    key_of = jax.random.split(jax.random.key(seed), 7)
    part_splits = jax.random.split(jax.random.fold_in(key_of[6], part), 7)
    return {
        "queries": scatter_about(part_splits[0], (TOKENS, HEADS * HD), 1.0, 6.0, ((0, 8), (1, 2))),
        "keys": scatter_about(part_splits[1], (TOKENS, KVH * HD), 1.0, 6.0, ((0, 8), (1, 2))),
        "values": draw_values(jax.random.fold_in(jax.random.fold_in(key_of[6], part), 71), part),
        "feat_weight": scatter_about(key_of[3], (HEADS, HD, HD), HD ** -0.5, 0.5, ((0, 2),)),
        "head_gain": jnp.clip(1.0 + 0.18 * jax.random.normal(key_of[4], (HEADS * HD,), jnp.float32), 0.1, 1.9),
        "out_weight": scatter_about(key_of[5], (HEADS * HD, DOUT), (HEADS * HD) ** -0.5, 0.09375, ((0, 2),)),
    }


def feature(inputs, feat_weight):
    mapped = jnp.einsum('thd,hde->the', inputs.astype(jnp.float32), feat_weight.astype(jnp.float32))
    return (jax.nn.elu(mapped) + 1.0).astype(jnp.bfloat16)

def reference(queries, keys, values, feat_weight, head_gain, out_weight):
    group_size = HEADS // KVH
    query_blocks = queries.reshape(N_SEQ, TOK_DEV, HEADS, HD)
    key_blocks = keys.reshape(N_SEQ, TOK_DEV, KVH, HD)
    value_blocks = values.reshape(N_SEQ, TOK_DEV, KVH, HD)
    gain_heads = head_gain.reshape(HEADS, HD).astype(jnp.float32)
    causal = jnp.arange(TOK_DEV)[:, None] >= jnp.arange(TOK_DEV)[None, :]

    def one_step(prefix, items):
        query_now, key_now, value_now = items
        feat_query = feature(query_now, feat_weight).astype(jnp.float32)
        feat_key = feature(jnp.repeat(key_now, group_size, axis=1), feat_weight).astype(jnp.float32)
        value_rep = jnp.repeat(value_now, group_size, axis=1).astype(jnp.float32)
        state_now = jnp.einsum('thf,thd->hfd', feat_key, value_rep)
        inter_part = jnp.einsum('thf,hfd->thd', feat_query, prefix, precision=lax.Precision.HIGHEST)
        scores = jnp.einsum('thf,shf->hts', feat_query, feat_key)
        scores = jnp.where(causal[None], scores, 0.0).astype(jnp.bfloat16).astype(jnp.float32)
        intra_part = jnp.einsum('hts,shd->thd', scores, value_rep)
        attn = inter_part + intra_part
        normed = attn * lax.rsqrt(lax.optimization_barrier(jnp.mean(attn * attn, axis=-1, keepdims=True)) + 1e-06) * gain_heads
        return (prefix + state_now, normed.astype(jnp.bfloat16).reshape(TOK_DEV, HEADS * HD))
    start = jnp.zeros((HEADS, HD, HD), jnp.float32)
    _, normed_all = lax.scan(one_step, start, (query_blocks, key_blocks, value_blocks))
    flat = normed_all.reshape(TOKENS, HEADS * HD)
    return jnp.dot(flat, out_weight, preferred_element_type=jnp.float32).astype(jnp.bfloat16)
```

```python
import functools

import jax
import jax.numpy as jnp
from jax import lax
from jax.experimental import pallas as pl
from jax.experimental.pallas import tpu as pltpu
from jax.sharding import PartitionSpec as P

HD = 128
PAIR = 2 * HD
COLS = 512
MESH = pl.DeviceIdType.MESH
NT = (((1,), (1,)), ((), ()))


def feature(mapped):
    return jnp.where(mapped > 0.0, mapped + 1.0, jnp.exp(jnp.minimum(mapped, 0.0))).astype(jnp.bfloat16)


def kernel(
    n_seq, q_hbm, k_hbm, v_hbm, fw_hbm, gain_hbm, w_hbm, out_hbm,
    q_buf, k_buf, v_buf, fw_buf, gain_buf, w_buf, out_buf,
    fk_buf, fq_buf, intra_buf, nrm_buf, acc,
    s_buf, peer_s, p_buf, fwd, mp_recv,
    q_sem, kv_sem, w_sem, out_sem,
    y_send, y_recv, z_send, z_recv, mp_send, mp_recv_sem,
):
    grp = lax.axis_index("groups")
    me = lax.axis_index("seq")
    mp = lax.axis_index("mp")
    layer = lax.div(me, 2)
    side = lax.rem(me, 2)
    mate = (grp, me + 1 - 2 * side, mp)
    up = (grp, me + 2, mp)
    down = (grp, me - 2, mp)
    other_mp = 1 - mp
    peer = (grp, me, other_mp)
    has_down = layer > 0
    has_up = me + 2 < n_seq
    n_pairs = q_buf.shape[0]
    rows = q_buf.shape[1]
    half = rows // 2
    n_cols = acc.shape[0]
    n_kv = k_buf.shape[1] // HD
    pairs_kv = n_pairs // n_kv

    def k_copy():
        return pltpu.make_async_copy(k_hbm, k_buf, kv_sem.at[0])

    def v_copy():
        return pltpu.make_async_copy(v_hbm, v_buf, kv_sem.at[1])

    def fw_copy():
        return pltpu.make_async_copy(fw_hbm, fw_buf, kv_sem.at[2])

    def gain_copy():
        return pltpu.make_async_copy(gain_hbm, gain_buf, kv_sem.at[3])

    def q_copy(i):
        at = pl.multiple_of(i * PAIR, PAIR)
        return pltpu.make_async_copy(q_hbm.at[:, pl.ds(at, PAIR)], q_buf.at[i], q_sem.at[i])

    def w_copy(i):
        at = pl.multiple_of(i * PAIR, PAIR)
        return pltpu.make_async_copy(w_hbm.at[pl.ds(at, PAIR), :], w_buf.at[i], w_sem.at[i])

    def y_copy(i):
        return pltpu.make_async_remote_copy(
            src_ref=s_buf.at[i], dst_ref=peer_s.at[i], send_sem=y_send.at[i],
            recv_sem=y_recv.at[i], device_id=mate, device_id_type=MESH)

    def z_copy(i):
        return pltpu.make_async_remote_copy(
            src_ref=fwd.at[i], dst_ref=p_buf.at[i], send_sem=z_send.at[i],
            recv_sem=z_recv.at[i], device_id=up, device_id_type=MESH)

    def mp_copy(c):
        return pltpu.make_async_remote_copy(
            src_ref=acc.at[c, pl.ds(pl.multiple_of(other_mp * half, half), half)],
            dst_ref=mp_recv.at[c], send_sem=mp_send.at[c],
            recv_sem=mp_recv_sem.at[c], device_id=peer, device_id_type=MESH)

    def out_copy(c):
        at = pl.multiple_of(c * COLS, COLS)
        return pltpu.make_async_copy(out_buf.at[c], out_hbm.at[:, pl.ds(at, COLS)], out_sem.at[c])

    k_copy().start()
    fw_copy().start()
    v_copy().start()
    gain_copy().start()

    @pl.loop(0, n_pairs)
    def _(i):
        q_copy(i).start()

    @pl.loop(0, n_pairs)
    def _(i):
        w_copy(i).start()

    barrier = pltpu.get_barrier_semaphore()
    pl.semaphore_signal(barrier, inc=1, device_id=mate, device_id_type=MESH)
    pl.semaphore_signal(barrier, inc=1, device_id=peer, device_id_type=MESH)

    @pl.when(has_up)
    def _():
        pl.semaphore_signal(barrier, inc=1, device_id=up, device_id_type=MESH)

    @pl.when(has_down)
    def _():
        pl.semaphore_signal(barrier, inc=1, device_id=down, device_id_type=MESH)

    pl.semaphore_wait(barrier, 2 + has_up.astype(jnp.int32) + has_down.astype(jnp.int32))

    @pl.when(jnp.logical_not(has_down))
    def _():
        p_buf[...] = jnp.zeros_like(p_buf)

    k_copy().wait()
    fw_copy().wait()
    v_copy().wait()

    for g in range(n_kv):
        keys = k_buf[:, g * HD:(g + 1) * HD]
        values_t = v_buf[:, g * HD:(g + 1) * HD].T

        @pl.loop(g * pairs_kv, (g + 1) * pairs_kv)
        def _(i):
            weight = jnp.concatenate([fw_buf[2 * i], fw_buf[2 * i + 1]], axis=1)
            fk = feature(jnp.dot(keys, weight, preferred_element_type=jnp.float32))
            fk_buf[i] = fk
            s_buf[i] = jnp.dot(values_t, fk, preferred_element_type=jnp.float32)
            y_copy(i).start()

    gain_copy().wait()

    def intra(i):
        q_copy(i).wait()
        zero = jnp.zeros((HD, HD), jnp.bfloat16)
        weight = jnp.concatenate(
            [jnp.concatenate([fw_buf[2 * i], zero], axis=1),
             jnp.concatenate([zero, fw_buf[2 * i + 1]], axis=1)], axis=0)
        fq = feature(jnp.dot(q_buf[i], weight, preferred_element_type=jnp.float32))
        fq_buf[i] = fq
        kv_at = pl.multiple_of(lax.div(i, pairs_kv) * HD, HD)
        values = v_buf[:, pl.ds(kv_at, HD)]
        causal = (lax.broadcasted_iota(jnp.int32, (half, half), 0)
                  >= lax.broadcasted_iota(jnp.int32, (half, half), 1))
        for j in range(2):
            lanes = slice(j * HD, (j + 1) * HD)
            fk_h = fk_buf[i, :, lanes]
            fq_h = fq[:, lanes]
            top = lax.dot_general(fq_h[:half], fk_h[:half], NT, preferred_element_type=jnp.float32)
            top = jnp.where(causal, top, 0.0).astype(jnp.bfloat16)
            intra_buf[i, :half, lanes] = jnp.dot(top, values[:half], preferred_element_type=jnp.float32)
            left = lax.dot_general(fq_h[half:], fk_h[:half], NT, preferred_element_type=jnp.float32)
            right = lax.dot_general(fq_h[half:], fk_h[half:], NT, preferred_element_type=jnp.float32)
            right = jnp.where(causal, right, 0.0)
            low = jnp.concatenate([left.astype(jnp.bfloat16), right.astype(jnp.bfloat16)], axis=1)
            intra_buf[i, half:, lanes] = jnp.dot(low, values, preferred_element_type=jnp.float32)

    def serve(i):
        y_copy(i).wait_recv()

        @pl.when(has_down)
        def _():
            z_copy(i).wait_recv()

        @pl.when(has_up)
        def _():
            fwd[i] = p_buf[i] + s_buf[i] + peer_s[i]
            z_copy(i).start()

    def finish(i):
        prefix = p_buf[i] + jnp.where(side == 1, peer_s[i], 0.0)
        high = prefix.astype(jnp.bfloat16)
        low = (prefix - high.astype(jnp.float32)).astype(jnp.bfloat16)
        for j in range(2):
            lanes = slice(j * HD, (j + 1) * HD)
            fq_h = fq_buf[i, :, lanes]
            inter = lax.dot_general(
                jnp.concatenate([fq_h, fq_h], axis=1),
                jnp.concatenate([high[:, lanes], low[:, lanes]], axis=1),
                NT, preferred_element_type=jnp.float32)
            attn = inter + intra_buf[i, :, lanes]
            scale = lax.rsqrt(jnp.mean(attn * attn, axis=-1, keepdims=True) + 1e-06)
            gain = gain_buf[pl.ds(2 * i + j, 1), :]
            nrm_buf[:, lanes] = (attn * scale * gain).astype(jnp.bfloat16)

    def project(i):
        w_copy(i).wait()

        @pl.when(i == 0)
        def _():
            @pl.loop(0, n_cols)
            def _(c):
                at = pl.multiple_of(c * COLS, COLS)
                acc[c] = jnp.dot(nrm_buf[...], w_buf[i, :, pl.ds(at, COLS)], preferred_element_type=jnp.float32)

        @pl.when(i > 0)
        def _():
            @pl.loop(0, n_cols)
            def _(c):
                at = pl.multiple_of(c * COLS, COLS)
                acc[c] += jnp.dot(nrm_buf[...], w_buf[i, :, pl.ds(at, COLS)], preferred_element_type=jnp.float32)

    last = n_pairs - 1

    @pl.loop(0, n_pairs + n_seq // 2 - 1)
    def _(t):
        @pl.when(t < n_pairs)
        def _():
            intra(t)

        i = t - layer

        @pl.when(jnp.logical_and(i >= 0, i < n_pairs))
        def _():
            serve(i)
            finish(i)

            @pl.when(i < last)
            def _():
                project(i)

    w_copy(last).wait()
    theirs = pl.ds(pl.multiple_of(other_mp * half, half), half)
    mine = pl.ds(pl.multiple_of(mp * half, half), half)

    @pl.loop(0, n_cols)
    def _(c):
        at = pl.multiple_of(c * COLS, COLS)
        acc[c, theirs] += jnp.dot(nrm_buf[theirs], w_buf[last, :, pl.ds(at, COLS)], preferred_element_type=jnp.float32)
        mp_copy(c).start()

    @pl.loop(0, n_cols)
    def _(c):
        at = pl.multiple_of(c * COLS, COLS)
        total = acc[c, mine] + jnp.dot(nrm_buf[mine], w_buf[last, :, pl.ds(at, COLS)], preferred_element_type=jnp.float32)
        mp_copy(c).wait_recv()
        out_buf[c] = (total + mp_recv[c]).astype(jnp.bfloat16)
        out_copy(c).start()

    @pl.loop(0, n_pairs)
    def _(i):
        y_copy(i).wait_send()

        @pl.when(has_up)
        def _():
            z_copy(i).wait_send()

    @pl.loop(0, n_cols)
    def _(c):
        mp_copy(c).wait_send()
        out_copy(c).wait()


def body(n_seq, queries, keys, values, feat_weight, head_gain, out_weight):
    rows, feats = queries.shape
    heads = feat_weight.shape[0]
    n_pairs = heads // 2
    dout = out_weight.shape[1]
    n_cols = dout // COLS
    half = rows // 2
    bf, f32 = jnp.bfloat16, jnp.float32
    gain = head_gain.reshape(heads, HD)
    dma = pltpu.SemaphoreType.DMA
    return pl.pallas_call(
        functools.partial(kernel, n_seq),
        out_shape=jax.ShapeDtypeStruct((half, dout), bf),
        in_specs=[pl.BlockSpec(memory_space=pl.ANY)] * 6,
        out_specs=pl.BlockSpec(memory_space=pl.ANY),
        scratch_shapes=[
            pltpu.VMEM((n_pairs, rows, PAIR), bf),
            pltpu.VMEM(keys.shape, bf),
            pltpu.VMEM(values.shape, bf),
            pltpu.VMEM(feat_weight.shape, bf),
            pltpu.VMEM((heads, HD), f32),
            pltpu.VMEM((n_pairs, PAIR, dout), bf),
            pltpu.VMEM((n_cols, half, COLS), bf),
            pltpu.VMEM((n_pairs, rows, PAIR), bf),
            pltpu.VMEM((n_pairs, rows, PAIR), bf),
            pltpu.VMEM((n_pairs, rows, PAIR), f32),
            pltpu.VMEM((rows, PAIR), bf),
            pltpu.VMEM((n_cols, rows, COLS), f32),
            pltpu.VMEM((n_pairs, HD, PAIR), f32),
            pltpu.VMEM((n_pairs, HD, PAIR), f32),
            pltpu.VMEM((n_pairs, HD, PAIR), f32),
            pltpu.VMEM((n_pairs, HD, PAIR), f32),
            pltpu.VMEM((n_cols, half, COLS), f32),
            dma((n_pairs,)), dma((4,)), dma((n_pairs,)), dma((n_cols,)),
            dma((n_pairs,)), dma((n_pairs,)), dma((n_pairs,)), dma((n_pairs,)),
            dma((n_cols,)), dma((n_cols,)),
        ],
        compiler_params=pltpu.CompilerParams(
            collective_id=0, has_side_effects=True, vmem_limit_bytes=60 * 1024 * 1024),
        cost_estimate=pl.CostEstimate(
            flops=2 * rows * feats * dout, bytes_accessed=feats * dout * 2, transcendentals=0),
    )(queries, keys, values, feat_weight, gain, out_weight)


def solution(mesh):
    return jax.shard_map(
        functools.partial(body, mesh.shape["seq"]),
        mesh=mesh,
        in_specs=(
            P(("groups", "seq"), "mp"),
            P(("groups", "seq"), "mp"),
            P(("groups", "seq"), "mp"),
            P("mp", None, None),
            P("mp"),
            P("mp", None),
        ),
        out_specs=P(("groups", "seq", "mp"), None),
        check_vma=False,
    )
```

```python
import functools

import jax
import jax.numpy as jnp
from jax import lax
from jax.experimental import pallas as pl
from jax.experimental.pallas import tpu as pltpu
from jax.sharding import PartitionSpec as P

HD = 128
PAIR = 2 * HD
COLS = 512
MESH = pl.DeviceIdType.MESH
NT = (((1,), (1,)), ((), ()))


def feature(mapped):
    return jnp.where(mapped > 0.0, mapped + 1.0, jnp.exp(jnp.minimum(mapped, 0.0))).astype(jnp.bfloat16)


def kernel(
    n_seq, q_hbm, k_hbm, v_hbm, fw_hbm, gain_hbm, w_hbm, out_hbm,
    q_buf, k_buf, v_buf, fw_buf, gain_buf, w_buf, out_buf,
    vt_buf, fk_buf, fq_buf, intra_buf, nrm_buf, acc,
    s_buf, peer_s, p_buf, fwd, pre_out, pre_in, mp_recv,
    q_sem, kv_sem, w_sem, out_sem,
    y_send, y_recv, z_send, z_recv, b_send, b_recv, mp_send, mp_recv_sem,
):
    grp = lax.axis_index("groups")
    me = lax.axis_index("seq")
    mp = lax.axis_index("mp")
    layer = lax.div(me, 2)
    side = lax.rem(me, 2)
    mate = (grp, me + 1 - 2 * side, mp)
    up = (grp, me + 2, mp)
    down = (grp, me - 2, mp)
    other_mp = 1 - mp
    peer = (grp, me, other_mp)
    has_down = layer > 0
    has_up = me + 2 < n_seq
    n_pairs = q_buf.shape[0]
    rows = q_buf.shape[1]
    half = rows // 2
    n_cols = acc.shape[0]
    n_kv = k_buf.shape[1] // HD
    pairs_kv = n_pairs // n_kv
    own_pairs = n_pairs // 2
    own_heads = 2 * own_pairs
    own_at = side * own_pairs
    mate_at = own_pairs - own_at

    def k_copy():
        return pltpu.make_async_copy(k_hbm, k_buf, kv_sem.at[0])

    def v_copy():
        return pltpu.make_async_copy(v_hbm, v_buf, kv_sem.at[1])

    def fw_copy():
        return pltpu.make_async_copy(fw_hbm, fw_buf, kv_sem.at[2])

    def gain_copy():
        return pltpu.make_async_copy(gain_hbm, gain_buf, kv_sem.at[3])

    def q_copy(i):
        at = pl.multiple_of(i * PAIR, PAIR)
        return pltpu.make_async_copy(q_hbm.at[:, pl.ds(at, PAIR)], q_buf.at[i], q_sem.at[i])

    def w_copy(i):
        at = pl.multiple_of(i * PAIR, PAIR)
        return pltpu.make_async_copy(w_hbm.at[pl.ds(at, PAIR), :], w_buf.at[lax.div(i, own_pairs), pl.ds(pl.multiple_of(lax.rem(i, own_pairs) * PAIR, PAIR), PAIR)], w_sem.at[i])

    def y_copy(i):
        return pltpu.make_async_remote_copy(
            src_ref=s_buf.at[2 * mate_at + i], dst_ref=peer_s.at[i], send_sem=y_send.at[i],
            recv_sem=y_recv.at[i], device_id=mate, device_id_type=MESH)

    def z_copy(i):
        return pltpu.make_async_remote_copy(
            src_ref=fwd.at[i], dst_ref=p_buf.at[i], send_sem=z_send.at[i],
            recv_sem=z_recv.at[i], device_id=up, device_id_type=MESH)

    def b_copy(i):
        return pltpu.make_async_remote_copy(
            src_ref=pre_out.at[i], dst_ref=pre_in.at[i], send_sem=b_send.at[i],
            recv_sem=b_recv.at[i], device_id=mate, device_id_type=MESH)

    def mp_copy(c):
        return pltpu.make_async_remote_copy(
            src_ref=acc.at[c, pl.ds(pl.multiple_of(other_mp * half, half), half)],
            dst_ref=mp_recv.at[c], send_sem=mp_send.at[c],
            recv_sem=mp_recv_sem.at[c], device_id=peer, device_id_type=MESH)

    def out_copy(c):
        at = pl.multiple_of(c * COLS, COLS)
        return pltpu.make_async_copy(out_buf.at[c], out_hbm.at[:, pl.ds(at, COLS)], out_sem.at[c])

    k_copy().start()
    fw_copy().start()
    v_copy().start()
    gain_copy().start()

    @pl.loop(0, n_pairs)
    def _(i):
        q_copy(i).start()

    @pl.loop(0, n_pairs)
    def _(i):
        w_copy(i).start()

    barrier = pltpu.get_barrier_semaphore()
    pl.semaphore_signal(barrier, inc=1, device_id=mate, device_id_type=MESH)
    pl.semaphore_signal(barrier, inc=1, device_id=peer, device_id_type=MESH)

    @pl.when(has_up)
    def _():
        pl.semaphore_signal(barrier, inc=1, device_id=up, device_id_type=MESH)

    @pl.when(has_down)
    def _():
        pl.semaphore_signal(barrier, inc=1, device_id=down, device_id_type=MESH)

    pl.semaphore_wait(barrier, 2 + has_up.astype(jnp.int32) + has_down.astype(jnp.int32))

    @pl.when(jnp.logical_not(has_down))
    def _():
        p_buf[...] = jnp.zeros_like(p_buf)

    k_copy().wait()
    fw_copy().wait()
    v_copy().wait()

    def states(i):
        kv_at = pl.multiple_of(lax.div(i, pairs_kv) * HD, HD)
        weight = jnp.concatenate([fw_buf[2 * i], fw_buf[2 * i + 1]], axis=1)
        fk = feature(jnp.dot(k_buf[:, pl.ds(kv_at, HD)], weight, preferred_element_type=jnp.float32))
        fk_buf[i] = fk
        state = jnp.dot(vt_buf[lax.div(i, pairs_kv)], fk, preferred_element_type=jnp.float32)
        s_buf[2 * i] = state[:, :HD]
        s_buf[2 * i + 1] = state[:, HD:]

    for g in range(n_kv):
        vt_buf[g] = v_buf[:, g * HD:(g + 1) * HD].T

    @pl.loop(0, own_pairs)
    def _(t):
        states(mate_at + t)
        y_copy(2 * t).start()
        y_copy(2 * t + 1).start()

    @pl.loop(0, own_pairs)
    def _(t):
        states(own_at + t)

    gain_copy().wait()

    def intra(i):
        q_copy(i).wait()
        zero = jnp.zeros((HD, HD), jnp.bfloat16)
        weight = jnp.concatenate(
            [jnp.concatenate([fw_buf[2 * i], zero], axis=1),
             jnp.concatenate([zero, fw_buf[2 * i + 1]], axis=1)], axis=0)
        fq = feature(jnp.dot(q_buf[i], weight, preferred_element_type=jnp.float32))
        fq_buf[i] = fq
        kv_at = pl.multiple_of(lax.div(i, pairs_kv) * HD, HD)
        values = v_buf[:, pl.ds(kv_at, HD)]
        causal = (lax.broadcasted_iota(jnp.int32, (half, half), 0)
                  >= lax.broadcasted_iota(jnp.int32, (half, half), 1))
        for j in range(2):
            lanes = slice(j * HD, (j + 1) * HD)
            fk_h = fk_buf[i, :, lanes]
            fq_h = fq[:, lanes]
            top = lax.dot_general(fq_h[:half], fk_h[:half], NT, preferred_element_type=jnp.float32)
            top = jnp.where(causal, top, 0.0).astype(jnp.bfloat16)
            intra_buf[i, :half, lanes] = jnp.dot(top, values[:half], preferred_element_type=jnp.float32)
            left = lax.dot_general(fq_h[half:], fk_h[:half], NT, preferred_element_type=jnp.float32)
            right = lax.dot_general(fq_h[half:], fk_h[half:], NT, preferred_element_type=jnp.float32)
            right = jnp.where(causal, right, 0.0)
            low = jnp.concatenate([left.astype(jnp.bfloat16), right.astype(jnp.bfloat16)], axis=1)
            intra_buf[i, half:, lanes] = jnp.dot(low, values, preferred_element_type=jnp.float32)

    def serve(k):
        y_copy(k).wait_recv()

        @pl.when(has_down)
        def _():
            z_copy(k).wait_recv()

        @pl.when(has_up)
        def _():
            fwd[k] = p_buf[k] + s_buf[2 * own_at + k] + peer_s[k]
            z_copy(k).start()

        pre_out[k] = p_buf[k] + jnp.where(side == 0, s_buf[2 * own_at + k], 0.0)
        b_copy(k).start()

    def finish(i, grp_at, prefixes):
        for j in range(2):
            lanes = slice(j * HD, (j + 1) * HD)
            high = prefixes[j].astype(jnp.bfloat16)
            low = (prefixes[j] - high.astype(jnp.float32)).astype(jnp.bfloat16)
            fq_h = fq_buf[i, :, lanes]
            inter = lax.dot_general(
                jnp.concatenate([fq_h, fq_h], axis=1),
                jnp.concatenate([high, low], axis=1),
                NT, preferred_element_type=jnp.float32)
            attn = inter + intra_buf[i, :, lanes]
            scale = lax.rsqrt(jnp.mean(attn * attn, axis=-1, keepdims=True) + 1e-06)
            gain = gain_buf[pl.ds(2 * i + j, 1), :]
            at = pl.multiple_of(lax.rem(i, own_pairs) * PAIR + j * HD, HD)
            nrm_buf[grp_at, :, pl.ds(at, HD)] = (attn * scale * gain).astype(jnp.bfloat16)

    def finish_own(m):
        finish(own_at + m, side, [
            p_buf[2 * m + j] + jnp.where(side == 1, peer_s[2 * m + j], 0.0) for j in range(2)])

    def finish_mate(m):
        b_copy(2 * m).wait_recv()
        b_copy(2 * m + 1).wait_recv()
        finish(mate_at + m, 1 - side, [pre_in[2 * m], pre_in[2 * m + 1]])

    @pl.loop(0, own_heads + n_seq // 2 - 1)
    def _(t):
        @pl.when(t < n_pairs)
        def _():
            intra(lax.rem(own_at + t, n_pairs))

        k = t - layer

        @pl.when(jnp.logical_and(k >= 0, k < own_heads))
        def _():
            serve(k)

            @pl.when(lax.rem(k, 2) == 1)
            def _():
                finish_own(lax.div(k, 2))

    @pl.loop(0, n_pairs)
    def _(i):
        w_copy(i).wait()

    cols_each = n_cols // own_pairs

    @pl.loop(0, own_pairs)
    def _(m):
        @pl.loop(m * cols_each, (m + 1) * cols_each)
        def _(c):
            at = pl.multiple_of(c * COLS, COLS)
            acc[c] = jnp.dot(nrm_buf[side], w_buf[side, :, pl.ds(at, COLS)], preferred_element_type=jnp.float32)

        finish_mate(m)

    theirs = pl.ds(pl.multiple_of(other_mp * half, half), half)
    mine = pl.ds(pl.multiple_of(mp * half, half), half)
    rest = 1 - side

    @pl.loop(0, n_cols)
    def _(c):
        at = pl.multiple_of(c * COLS, COLS)
        acc[c, theirs] += jnp.dot(nrm_buf[rest, theirs], w_buf[rest, :, pl.ds(at, COLS)], preferred_element_type=jnp.float32)
        mp_copy(c).start()

    @pl.loop(0, n_cols)
    def _(c):
        at = pl.multiple_of(c * COLS, COLS)
        total = acc[c, mine] + jnp.dot(nrm_buf[rest, mine], w_buf[rest, :, pl.ds(at, COLS)], preferred_element_type=jnp.float32)
        mp_copy(c).wait_recv()
        out_buf[c] = (total + mp_recv[c]).astype(jnp.bfloat16)
        out_copy(c).start()

    @pl.loop(0, own_heads)
    def _(i):
        y_copy(i).wait_send()
        b_copy(i).wait_send()

        @pl.when(has_up)
        def _():
            z_copy(i).wait_send()

    @pl.loop(0, n_cols)
    def _(c):
        mp_copy(c).wait_send()
        out_copy(c).wait()


def body(n_seq, queries, keys, values, feat_weight, head_gain, out_weight):
    rows, feats = queries.shape
    heads = feat_weight.shape[0]
    n_pairs = heads // 2
    dout = out_weight.shape[1]
    n_cols = dout // COLS
    half = rows // 2
    bf, f32 = jnp.bfloat16, jnp.float32
    gain = head_gain.reshape(heads, HD)
    dma = pltpu.SemaphoreType.DMA
    return pl.pallas_call(
        functools.partial(kernel, n_seq),
        out_shape=jax.ShapeDtypeStruct((half, dout), bf),
        in_specs=[pl.BlockSpec(memory_space=pl.ANY)] * 6,
        out_specs=pl.BlockSpec(memory_space=pl.ANY),
        scratch_shapes=[
            pltpu.VMEM((n_pairs, rows, PAIR), bf),
            pltpu.VMEM(keys.shape, bf),
            pltpu.VMEM(values.shape, bf),
            pltpu.VMEM(feat_weight.shape, bf),
            pltpu.VMEM((heads, HD), f32),
            pltpu.VMEM((2, feats // 2, dout), bf),
            pltpu.VMEM((n_cols, half, COLS), bf),
            pltpu.VMEM((keys.shape[1] // HD, HD, rows), bf),
            pltpu.VMEM((n_pairs, rows, PAIR), bf),
            pltpu.VMEM((n_pairs, rows, PAIR), bf),
            pltpu.VMEM((n_pairs, rows, PAIR), f32),
            pltpu.VMEM((2, rows, feats // 2), bf),
            pltpu.VMEM((n_cols, rows, COLS), f32),
            pltpu.VMEM((heads, HD, HD), f32),
            pltpu.VMEM((n_pairs, HD, HD), f32),
            pltpu.VMEM((n_pairs, HD, HD), f32),
            pltpu.VMEM((n_pairs, HD, HD), f32),
            pltpu.VMEM((n_pairs, HD, HD), f32),
            pltpu.VMEM((n_pairs, HD, HD), f32),
            pltpu.VMEM((n_cols, half, COLS), f32),
            dma((n_pairs,)), dma((4,)), dma((n_pairs,)), dma((n_cols,)),
            dma((n_pairs,)), dma((n_pairs,)), dma((n_pairs,)), dma((n_pairs,)),
            dma((n_pairs,)), dma((n_pairs,)),
            dma((n_cols,)), dma((n_cols,)),
        ],
        compiler_params=pltpu.CompilerParams(
            collective_id=0, has_side_effects=True, vmem_limit_bytes=60 * 1024 * 1024),
        cost_estimate=pl.CostEstimate(
            flops=2 * rows * feats * dout, bytes_accessed=feats * dout * 2, transcendentals=0),
    )(queries, keys, values, feat_weight, gain, out_weight)


def solution(mesh):
    return jax.shard_map(
        functools.partial(body, mesh.shape["seq"]),
        mesh=mesh,
        in_specs=(
            P(("groups", "seq"), "mp"),
            P(("groups", "seq"), "mp"),
            P(("groups", "seq"), "mp"),
            P("mp", None, None),
            P("mp"),
            P("mp", None),
        ),
        out_specs=P(("groups", "seq", "mp"), None),
        check_vma=False,
    )
```

```python
import functools

import jax
import jax.numpy as jnp
from jax import lax
from jax.experimental import pallas as pl
from jax.experimental.pallas import tpu as pltpu
from jax.sharding import PartitionSpec as P

HD = 128
PAIR = 2 * HD
COLS = 512
MESH = pl.DeviceIdType.MESH
NT = (((1,), (1,)), ((), ()))


def feature(mapped):
    return jnp.where(mapped > 0.0, mapped + 1.0, jnp.exp(jnp.minimum(mapped, 0.0))).astype(jnp.bfloat16)


def kernel(
    n_seq, q_hbm, k_hbm, v_hbm, fw_hbm, gain_hbm, w_hbm, out_ref,
    q_buf, k_buf, v_buf, fw_buf, gain_buf, w_buf,
    vt_buf, fk_buf, fq_buf, intra_buf, nrm_buf, acc,
    s_buf, peer_s, p_buf, fwd, pre_out, pre_in, mp_recv,
    q_sem, kv_sem, w_sem,
    y_send, y_recv, z_send, z_recv, b_send, b_recv, mp_send, mp_recv_sem,
):
    grp = lax.axis_index("groups")
    me = lax.axis_index("seq")
    mp = lax.axis_index("mp")
    layer = lax.div(me, 2)
    side = lax.rem(me, 2)
    mate = (grp, me + 1 - 2 * side, mp)
    up = (grp, me + 2, mp)
    down = (grp, me - 2, mp)
    other_mp = 1 - mp
    peer = (grp, me, other_mp)
    has_down = layer > 0
    has_up = me + 2 < n_seq
    n_pairs = q_buf.shape[0]
    rows = q_buf.shape[1]
    half = rows // 2
    n_cols = acc.shape[0]
    n_kv = k_buf.shape[1] // HD
    pairs_kv = n_pairs // n_kv
    own_pairs = n_pairs // 2
    own_heads = 2 * own_pairs
    own_at = side * own_pairs
    mate_at = own_pairs - own_at

    def k_copy():
        return pltpu.make_async_copy(k_hbm, k_buf, kv_sem.at[0])

    def v_copy():
        return pltpu.make_async_copy(v_hbm, v_buf, kv_sem.at[1])

    def fw_copy():
        return pltpu.make_async_copy(fw_hbm, fw_buf, kv_sem.at[2])

    def gain_copy():
        return pltpu.make_async_copy(gain_hbm, gain_buf, kv_sem.at[3])

    def q_copy(i):
        at = pl.multiple_of(i * PAIR, PAIR)
        return pltpu.make_async_copy(q_hbm.at[:, pl.ds(at, PAIR)], q_buf.at[i], q_sem.at[i])

    def w_copy(i):
        at = pl.multiple_of(i * PAIR, PAIR)
        return pltpu.make_async_copy(w_hbm.at[pl.ds(at, PAIR), :], w_buf.at[lax.div(i, own_pairs), pl.ds(pl.multiple_of(lax.rem(i, own_pairs) * PAIR, PAIR), PAIR)], w_sem.at[i])

    def y_copy(i):
        return pltpu.make_async_remote_copy(
            src_ref=s_buf.at[2 * mate_at + i], dst_ref=peer_s.at[i], send_sem=y_send.at[i],
            recv_sem=y_recv.at[i], device_id=mate, device_id_type=MESH)

    def z_copy(i):
        return pltpu.make_async_remote_copy(
            src_ref=fwd.at[i], dst_ref=p_buf.at[i], send_sem=z_send.at[i],
            recv_sem=z_recv.at[i], device_id=up, device_id_type=MESH)

    def b_copy(i):
        return pltpu.make_async_remote_copy(
            src_ref=pre_out.at[i], dst_ref=pre_in.at[i], send_sem=b_send.at[i],
            recv_sem=b_recv.at[i], device_id=mate, device_id_type=MESH)

    def mp_copy(c):
        return pltpu.make_async_remote_copy(
            src_ref=acc.at[c, pl.ds(pl.multiple_of(other_mp * half, half), half)],
            dst_ref=mp_recv.at[c], send_sem=mp_send.at[c],
            recv_sem=mp_recv_sem.at[c], device_id=peer, device_id_type=MESH)

    k_copy().start()
    fw_copy().start()
    v_copy().start()
    gain_copy().start()

    @pl.loop(0, n_pairs)
    def _(i):
        q_copy(i).start()

    @pl.loop(0, n_pairs)
    def _(i):
        w_copy(i).start()

    barrier = pltpu.get_barrier_semaphore()
    pl.semaphore_signal(barrier, inc=1, device_id=mate, device_id_type=MESH)
    pl.semaphore_signal(barrier, inc=1, device_id=peer, device_id_type=MESH)

    @pl.when(has_up)
    def _():
        pl.semaphore_signal(barrier, inc=1, device_id=up, device_id_type=MESH)

    @pl.when(has_down)
    def _():
        pl.semaphore_signal(barrier, inc=1, device_id=down, device_id_type=MESH)

    pl.semaphore_wait(barrier, 2 + has_up.astype(jnp.int32) + has_down.astype(jnp.int32))

    @pl.when(jnp.logical_not(has_down))
    def _():
        p_buf[...] = jnp.zeros_like(p_buf)

    k_copy().wait()
    fw_copy().wait()
    v_copy().wait()

    def states(i):
        kv_at = pl.multiple_of(lax.div(i, pairs_kv) * HD, HD)
        weight = jnp.concatenate([fw_buf[2 * i], fw_buf[2 * i + 1]], axis=1)
        fk = feature(jnp.dot(k_buf[:, pl.ds(kv_at, HD)], weight, preferred_element_type=jnp.float32))
        fk_buf[i] = fk
        state = jnp.dot(vt_buf[lax.div(i, pairs_kv)], fk, preferred_element_type=jnp.float32)
        s_buf[2 * i] = state[:, :HD]
        s_buf[2 * i + 1] = state[:, HD:]

    for g in range(n_kv):
        vt_buf[g] = v_buf[:, g * HD:(g + 1) * HD].T

    @pl.loop(0, own_pairs)
    def _(t):
        states(mate_at + t)
        y_copy(2 * t).start()
        y_copy(2 * t + 1).start()

    @pl.loop(0, own_pairs)
    def _(t):
        states(own_at + t)

    gain_copy().wait()

    def intra(i):
        q_copy(i).wait()
        zero = jnp.zeros((HD, HD), jnp.bfloat16)
        weight = jnp.concatenate(
            [jnp.concatenate([fw_buf[2 * i], zero], axis=1),
             jnp.concatenate([zero, fw_buf[2 * i + 1]], axis=1)], axis=0)
        fq = feature(jnp.dot(q_buf[i], weight, preferred_element_type=jnp.float32))
        fq_buf[i] = fq
        kv_at = pl.multiple_of(lax.div(i, pairs_kv) * HD, HD)
        values = v_buf[:, pl.ds(kv_at, HD)]
        causal = (lax.broadcasted_iota(jnp.int32, (half, half), 0)
                  >= lax.broadcasted_iota(jnp.int32, (half, half), 1))
        for j in range(2):
            lanes = slice(j * HD, (j + 1) * HD)
            fk_h = fk_buf[i, :, lanes]
            fq_h = fq[:, lanes]
            top = lax.dot_general(fq_h[:half], fk_h[:half], NT, preferred_element_type=jnp.float32)
            top = jnp.where(causal, top, 0.0).astype(jnp.bfloat16)
            intra_buf[i, :half, lanes] = jnp.dot(top, values[:half], preferred_element_type=jnp.float32)
            left = lax.dot_general(fq_h[half:], fk_h[:half], NT, preferred_element_type=jnp.float32)
            right = lax.dot_general(fq_h[half:], fk_h[half:], NT, preferred_element_type=jnp.float32)
            right = jnp.where(causal, right, 0.0)
            low = jnp.concatenate([left.astype(jnp.bfloat16), right.astype(jnp.bfloat16)], axis=1)
            intra_buf[i, half:, lanes] = jnp.dot(low, values, preferred_element_type=jnp.float32)

    def serve(k):
        y_copy(k).wait_recv()

        @pl.when(has_down)
        def _():
            z_copy(k).wait_recv()

        @pl.when(has_up)
        def _():
            fwd[k] = p_buf[k] + s_buf[2 * own_at + k] + peer_s[k]
            z_copy(k).start()

        pre_out[k] = p_buf[k] + jnp.where(side == 0, s_buf[2 * own_at + k], 0.0)
        b_copy(k).start()

    def finish(i, grp_at, prefixes):
        for j in range(2):
            lanes = slice(j * HD, (j + 1) * HD)
            high = prefixes[j].astype(jnp.bfloat16)
            low = (prefixes[j] - high.astype(jnp.float32)).astype(jnp.bfloat16)
            fq_h = fq_buf[i, :, lanes]
            inter = lax.dot_general(
                jnp.concatenate([fq_h, fq_h], axis=1),
                jnp.concatenate([high, low], axis=1),
                NT, preferred_element_type=jnp.float32)
            attn = inter + intra_buf[i, :, lanes]
            scale = lax.rsqrt(jnp.mean(attn * attn, axis=-1, keepdims=True) + 1e-06)
            gain = gain_buf[pl.ds(2 * i + j, 1), :]
            at = pl.multiple_of(lax.rem(i, own_pairs) * PAIR + j * HD, HD)
            nrm_buf[grp_at, :, pl.ds(at, HD)] = (attn * scale * gain).astype(jnp.bfloat16)

    def finish_own(m):
        finish(own_at + m, side, [
            p_buf[2 * m + j] + jnp.where(side == 1, peer_s[2 * m + j], 0.0) for j in range(2)])

    def finish_mate(m):
        b_copy(2 * m).wait_recv()
        b_copy(2 * m + 1).wait_recv()
        finish(mate_at + m, 1 - side, [pre_in[2 * m], pre_in[2 * m + 1]])

    @pl.loop(0, own_heads + n_seq // 2 - 1)
    def _(t):
        @pl.when(t < n_pairs)
        def _():
            intra(lax.rem(own_at + t, n_pairs))

        k = t - layer

        @pl.when(jnp.logical_and(k >= 0, k < own_heads))
        def _():
            serve(k)

            @pl.when(lax.rem(k, 2) == 1)
            def _():
                finish_own(lax.div(k, 2))

    @pl.loop(0, n_pairs)
    def _(i):
        w_copy(i).wait()

    cols_each = n_cols // own_pairs

    @pl.loop(0, own_pairs)
    def _(m):
        @pl.loop(m * cols_each, (m + 1) * cols_each)
        def _(c):
            at = pl.multiple_of(c * COLS, COLS)
            acc[c] = jnp.dot(nrm_buf[side], w_buf[side, :, pl.ds(at, COLS)], preferred_element_type=jnp.float32)

        finish_mate(m)

    theirs = pl.ds(pl.multiple_of(other_mp * half, half), half)
    mine = pl.ds(pl.multiple_of(mp * half, half), half)
    rest = 1 - side

    @pl.loop(0, n_cols)
    def _(c):
        at = pl.multiple_of(c * COLS, COLS)
        acc[c, theirs] += jnp.dot(nrm_buf[rest, theirs], w_buf[rest, :, pl.ds(at, COLS)], preferred_element_type=jnp.float32)
        mp_copy(c).start()

    @pl.loop(0, n_cols)
    def _(c):
        at = pl.multiple_of(c * COLS, COLS)
        total = acc[c, mine] + jnp.dot(nrm_buf[rest, mine], w_buf[rest, :, pl.ds(at, COLS)], preferred_element_type=jnp.float32)
        mp_copy(c).wait_recv()
        out_ref[:, pl.ds(at, COLS)] = (total + mp_recv[c]).astype(jnp.bfloat16)

    @pl.loop(0, own_heads)
    def _(i):
        y_copy(i).wait_send()
        b_copy(i).wait_send()

        @pl.when(has_up)
        def _():
            z_copy(i).wait_send()

    @pl.loop(0, n_cols)
    def _(c):
        mp_copy(c).wait_send()


def body(n_seq, queries, keys, values, feat_weight, head_gain, out_weight):
    rows, feats = queries.shape
    heads = feat_weight.shape[0]
    n_pairs = heads // 2
    dout = out_weight.shape[1]
    n_cols = dout // COLS
    half = rows // 2
    bf, f32 = jnp.bfloat16, jnp.float32
    gain = head_gain.reshape(heads, HD)
    dma = pltpu.SemaphoreType.DMA
    return pl.pallas_call(
        functools.partial(kernel, n_seq),
        out_shape=pltpu.VMEM((half, dout), bf),
        in_specs=[pl.BlockSpec(memory_space=pl.ANY)] * 6,
        out_specs=pl.BlockSpec(memory_space=pltpu.VMEM),
        scratch_shapes=[
            pltpu.VMEM((n_pairs, rows, PAIR), bf),
            pltpu.VMEM(keys.shape, bf),
            pltpu.VMEM(values.shape, bf),
            pltpu.VMEM(feat_weight.shape, bf),
            pltpu.VMEM((heads, HD), f32),
            pltpu.VMEM((2, feats // 2, dout), bf),
            pltpu.VMEM((keys.shape[1] // HD, HD, rows), bf),
            pltpu.VMEM((n_pairs, rows, PAIR), bf),
            pltpu.VMEM((n_pairs, rows, PAIR), bf),
            pltpu.VMEM((n_pairs, rows, PAIR), f32),
            pltpu.VMEM((2, rows, feats // 2), bf),
            pltpu.VMEM((n_cols, rows, COLS), f32),
            pltpu.VMEM((heads, HD, HD), f32),
            pltpu.VMEM((n_pairs, HD, HD), f32),
            pltpu.VMEM((n_pairs, HD, HD), f32),
            pltpu.VMEM((n_pairs, HD, HD), f32),
            pltpu.VMEM((n_pairs, HD, HD), f32),
            pltpu.VMEM((n_pairs, HD, HD), f32),
            pltpu.VMEM((n_cols, half, COLS), f32),
            dma((n_pairs,)), dma((4,)), dma((n_pairs,)),
            dma((n_pairs,)), dma((n_pairs,)), dma((n_pairs,)), dma((n_pairs,)),
            dma((n_pairs,)), dma((n_pairs,)),
            dma((n_cols,)), dma((n_cols,)),
        ],
        compiler_params=pltpu.CompilerParams(
            collective_id=0, has_side_effects=True, vmem_limit_bytes=58 * 1024 * 1024),
        cost_estimate=pl.CostEstimate(
            flops=2 * rows * feats * dout, bytes_accessed=feats * dout * 2, transcendentals=0),
    )(queries, keys, values, feat_weight, gain, out_weight)


def solution(mesh):
    return jax.shard_map(
        functools.partial(body, mesh.shape["seq"]),
        mesh=mesh,
        in_specs=(
            P(("groups", "seq"), "mp"),
            P(("groups", "seq"), "mp"),
            P(("groups", "seq"), "mp"),
            P("mp", None, None),
            P("mp"),
            P("mp", None),
        ),
        out_specs=P(("groups", "seq", "mp"), None),
        check_vma=False,
    )
```
